32 devices in a mesh: leaf: 16 (over z, y, x), rhs: 2 (over core).
Axes of the slice: x: 2, y: 2, z: 4, core: 2. Of those that a mesh axis runs over, the one named last changes fastest.
Arguments:
- points: bfloat16 [2048, 8, 256], P('leaf'), may hold values from -5 to 5
- values: bfloat16 [2048, 16, 256], P('leaf', 'rhs'), parts along dimension 1, may hold values from -6 to 6
- counts: int32 [2048], P('leaf'), may hold values from 128 to 256
- leaf_basis: bfloat16 [2048, 64, 256], P('leaf'), may hold values from -0.375 to 0.375
- transfer: bfloat16 [2048, 64, 64], P('leaf'), may hold values from -0.5 to 0.5
- leaf_skeleton: bfloat16 [2048, 8, 64], P('leaf'), may hold values from -5 to 5
- upper_skeleton: bfloat16 [1024, 8, 64], P('leaf'), may hold values from -5 to 5
- near_list: int32 [2048, 6], P('leaf'), may hold values from 0 to 2047, as said below
- far_owner: int32 [2048, 8], P('leaf'), may hold values from 0 to 15, all different within a row; in each aligned block of 128 rows (0 to 127, 128 to 255, ...) at most 128 rows name the same one
- far_local: int32 [2048, 8], P('leaf'), may hold values from 0 to 127
- upper_owner: int32 [1024, 8], P('leaf'), may hold values from 0 to 15, all different within a row; in each aligned block of 64 rows (0 to 63, 64 to 127, ...) at most 64 rows name the same one
- upper_local: int32 [1024, 8], P('leaf'), may hold values from 0 to 63
Outputs:
- product: float32 [2048, 16, 256], P('leaf', 'rhs'), parts along dimension 1
The draws below stay inside these ranges and needn't reach their ends.
There are 2 independent parts, one for each index of `rhs`. The reference program is written for one: setup_inputs(seed, part) draws one part's arguments, and reference() takes and returns one part's arrays. A program takes and returns all parts, laid end to end along the dimension named above; an argument that names none is the same for every part. Nothing has to cross between parts.
Inputs may be any that keep to these rules, and one draw needn't show every extreme that they name: `near_list`: entry 0 of leaf l's list is l itself; every entry lies within 4 leaves of the block of 128 leaves that holds l, and some lists reach both ends of that range where the grid of leaves allows. `far_owner`: A row's 8 owners are different; among the rows of one device (aligned blocks of 128 rows) no owner is named by more than 128 entries, and some owner by exactly that many. `upper_owner`: A row's 8 owners are different; among the rows of one device (aligned blocks of 64 rows) no owner is named by more than 64 entries, and some owner by exactly that many.
All inputs are finite; a program needn't handle non-finite values.
Results may differ from the reference program's by a relative error of at most 0.0032.
Values may be sent and summed in bfloat16 or wider, within the bound.
A program may use at most 128 MiB of HBM per device.

```python
import math
import jax
import jax.numpy as jnp
import numpy as np
from jax import lax

LEAF = 256
RANK = 64
DIM = 8
C = 8
LEAF_DEV = 128
NEAR = 6
FAR = 8
HALO = 4
OWNERS = 16
PAR_DEV = 64
LEAVES = 2048
PARENTS = 1024
CAP_LEAF = 128
CAP_UPPER = 64


def draw_near_list(key, part):
    key = jax.random.fold_in(key, 11)
    rows = jnp.arange(LEAVES, dtype=jnp.int32)
    start = rows // LEAF_DEV * LEAF_DEV
    offsets = jax.random.randint(key, (LEAVES, NEAR), -HALO, LEAF_DEV + HALO)
    picks = start[:, None] + offsets
    position = rows % LEAF_DEV
    lowest = jnp.where(position == 0, start - HALO, picks[:, 1])
    second = jnp.where(position == LEAF_DEV - 1, start + LEAF_DEV + HALO - 1, lowest)
    picks = picks.at[:, 1].set(second)
    picks = picks.at[:, 0].set(rows)
    return jnp.clip(picks, 0, LEAVES - 1).astype(jnp.int32)


def with_ends(array, stream_key, least, top_value):
    index_at = [jax.random.randint(jax.random.fold_in(stream_key, axis), (), 0, length) for axis, length in enumerate(array.shape)]
    widest = array.shape.index(max(array.shape))
    neighbour = index_at[:widest] + [(index_at[widest] + 1) % array.shape[widest]] + index_at[widest + 1:]
    return array.at[tuple(index_at)].set(least).at[tuple(neighbour)].set(top_value)


def levels(own_key, extent, split, least, largest):
    factor_of, own = 1.0, jax.random.fold_in(own_key, 6)
    for axis_at, blocks in split:
        heights = jnp.exp(jax.random.uniform(jax.random.fold_in(own, axis_at), (blocks,), jnp.float32, least / len(split), largest / len(split)))
        factor_of = factor_of * jnp.repeat(heights, extent[axis_at] // blocks).reshape([-1 if axis == axis_at else 1 for axis in range(len(extent))])
    return factor_of


def assign_block(rng, own, number, rows, number_of, top, reach, lean):
    order = jax.random.permutation(rng, number_of)
    packed, ordinary = portions_of(number_of, rows * top, reach, lean, True), portions_of(number_of, rows * top, reach, lean, False)
    places = jnp.arange(number_of)

    def named(sizes, offset_by):
        used = int((sizes > 0).sum())
        fixed = max(1, used // 4)
        passed = fixed + (places - fixed + offset_by * (used - fixed)) % max(1, number_of - fixed)
        return jnp.zeros((number_of,), jnp.int32).at[order[jnp.where(places < fixed, places, passed)]].set(jnp.asarray(sizes, jnp.int32))

    sizes = jnp.where(number % 4 == 0, named(packed, number // 4), named(ordinary, number - number // 4 - 1))
    mixed = jax.random.permutation(jax.random.fold_in(own, 3), number_of)
    source_of, receiver = mixed[0:number_of // 2 * 2:2], mixed[1:number_of // 2 * 2:2]
    slack = jnp.minimum(sizes[source_of] - 1, reach - sizes[receiver]) // 2
    slack = jnp.where((source_of == order[0]) | (receiver == order[0]) | (sizes[receiver] == 0), 0, jnp.maximum(slack, 0))
    passed = jax.random.randint(jax.random.fold_in(own, 4), (number_of // 2,), 0, 1 << 20) % (slack + 1)
    sizes = sizes.at[source_of].add(-passed).at[receiver].add(passed)
    items = jnp.searchsorted(jnp.cumsum(sizes), jnp.arange(rows * top), side="right").astype(jnp.int32)
    listing = items.reshape(top, rows).T
    listing = listing[jax.random.permutation(jax.random.fold_in(own, 1), rows)]
    offset_by = jax.random.randint(jax.random.fold_in(own, 2), (rows, 1), 0, top)
    return jnp.take_along_axis(listing, (jnp.arange(top)[None, :] + offset_by) % top, axis=1)


def portions_of(amount, total, reach, skew, full):
    weights = [(1 << 20) // math.isqrt(grade ** skew) + 1 for grade in range(1, amount + 1)]
    largest = reach if full else min(reach, max(-(-total // amount), total * weights[0] // sum(weights)))
    least = 1 if total - largest >= amount - 1 else 0
    given, rest = [largest] + [least] * (amount - 1), total - largest - least * (amount - 1)
    while rest > 0:
        candidates = [i for i in range(1, amount) if given[i] < largest] or [i for i in range(1, amount) if given[i] < reach]
        mass, left = sum([weights[i] for i in candidates]), rest
        for i in candidates:
            addition = min(reach - given[i], max(1, left * weights[i] // mass), rest)
            given[i] = given[i] + addition
            rest = rest - addition
    return np.array(given)


def normal_values(own_key, extent, scale, bound, split=(), kind=jnp.bfloat16):
    loudness = levels(own_key, extent, split, -0.22, 0.18) if split else 1.0
    array = jax.random.normal(own_key, extent, jnp.float32) * scale * loudness
    return jnp.minimum(jnp.maximum(array, -bound), bound).astype(kind)


def setup_inputs(seed: int = 0, part: int = 0) -> dict:
    streams_of = jax.random.split(jax.random.key(seed), 13)
    part_splits = jax.random.split(jax.random.fold_in(streams_of[12], part), 13)
    points = normal_values(streams_of[0], (LEAVES, DIM, LEAF), 1.0, 5.0, ((0, 16),))
    values = normal_values(part_splits[1], (LEAVES, C, LEAF), 1.0, 6.0, ((0, 16),))
    counts = with_ends(jax.random.randint(streams_of[2], (LEAVES,), LEAF // 2, LEAF + 1), jax.random.fold_in(streams_of[2], 1), LEAF // 2, LEAF).astype(jnp.int32)
    leaf_basis = normal_values(streams_of[3], (LEAVES, RANK, LEAF), LEAF ** -0.5, 0.375, ((0, 16),))
    transfer = normal_values(streams_of[4], (LEAVES, RANK, RANK), (2 * RANK) ** -0.5, 0.5, ((0, 16),))
    leaf_skeleton = normal_values(streams_of[5], (LEAVES, DIM, RANK), 1.0, 5.0, ((0, 16),))
    upper_skeleton = normal_values(streams_of[6], (PARENTS, DIM, RANK), 1.0, 5.0, ((0, 16),))
    near_list = draw_near_list(jax.random.fold_in(streams_of[12], 71), part)
    far_owner_keys = jax.random.split(jax.random.fold_in(streams_of[8], 1), LEAVES // LEAF_DEV)
    far_owner_turns = jax.random.permutation(jax.random.fold_in(streams_of[8], 3), LEAVES // LEAF_DEV)
    far_owner = jax.vmap(lambda own, number: assign_block(jax.random.fold_in(streams_of[8], 2), own, number, LEAF_DEV, OWNERS, FAR, CAP_LEAF, 2))(far_owner_keys, far_owner_turns).reshape((LEAVES, FAR))
    far_local = with_ends(jax.random.randint(streams_of[9], (LEAVES, FAR), 0, LEAF_DEV), jax.random.fold_in(streams_of[9], 1), 0, LEAF_DEV - 1).astype(jnp.int32)
    upper_owner_keys = jax.random.split(jax.random.fold_in(streams_of[10], 1), PARENTS // PAR_DEV)
    upper_owner_turns = jax.random.permutation(jax.random.fold_in(streams_of[10], 3), PARENTS // PAR_DEV)
    upper_owner = jax.vmap(lambda own, number: assign_block(jax.random.fold_in(streams_of[10], 2), own, number, PAR_DEV, OWNERS, FAR, CAP_UPPER, 2))(upper_owner_keys, upper_owner_turns).reshape((PARENTS, FAR))
    upper_local = with_ends(jax.random.randint(streams_of[11], (PARENTS, FAR), 0, PAR_DEV), jax.random.fold_in(streams_of[11], 1), 0, PAR_DEV - 1).astype(jnp.int32)
    return dict(points=points, values=values, counts=counts, leaf_basis=leaf_basis, transfer=transfer, leaf_skeleton=leaf_skeleton, upper_skeleton=upper_skeleton, near_list=near_list, far_owner=far_owner, far_local=far_local, upper_owner=upper_owner, upper_local=upper_local)


SQRT_THREE = 1.7320508075688772
LENGTH_SCALE = 1.5

def matern(targets, sources):
    square = 0.0
    for coord in range(targets.shape[-2]):
        offset = targets[..., coord, :, None] - sources[..., coord, None, :]
        square = square + offset * offset
    scaled = SQRT_THREE / LENGTH_SCALE * jnp.sqrt(square)
    return (1.0 + scaled) * jnp.exp(-scaled)

def blocked(single, arrays, group):
    count = arrays[0].shape[0]
    shaped = tuple((item.reshape((count // group, group) + item.shape[1:]) for item in arrays))
    mapped = lax.map(lambda pieces: jax.vmap(single)(*pieces), shaped)
    return mapped.reshape((count,) + mapped.shape[2:])

def far_field(skeleton, coefs, source_ids, group):

    def single(target_skel, chosen):
        kernel = matern(target_skel.astype(jnp.float32)[None], skeleton[chosen].astype(jnp.float32)).astype(jnp.bfloat16)
        return jnp.einsum('fcb,fab->ca', coefs[chosen].astype(jnp.float32), kernel.astype(jnp.float32))
    return blocked(single, (skeleton, source_ids), group)

def reference(points, values, counts, leaf_basis, transfer, leaf_skeleton, upper_skeleton, near_list, far_owner, far_local, upper_owner, upper_local):
    leaf_size = points.shape[2]
    point_live = jnp.arange(leaf_size, dtype=jnp.int32)[None, :] < counts[:, None]
    masked = jnp.where(point_live[:, None, :], values, jnp.zeros_like(values))
    leaf_coef = jnp.einsum('lcp,lkp->lck', masked.astype(jnp.float32), leaf_basis.astype(jnp.float32)).astype(jnp.bfloat16)
    pairs = leaf_coef.shape[0] // 2
    child_coef = leaf_coef.reshape((pairs, 2) + leaf_coef.shape[1:]).astype(jnp.float32)
    child_transfer = transfer.reshape((pairs, 2) + transfer.shape[1:]).astype(jnp.float32)
    upper_coef = jnp.einsum('pjck,pjkm->pcm', child_coef, child_transfer).astype(jnp.bfloat16)
    upper_ids = (upper_owner * PAR_DEV + upper_local).astype(jnp.int32)
    leaf_ids = (far_owner * LEAF_DEV + far_local).astype(jnp.int32)
    upper_field = far_field(upper_skeleton, upper_coef, upper_ids, PAR_DEV).astype(jnp.bfloat16)
    leaf_far = far_field(leaf_skeleton, leaf_coef, leaf_ids, LEAF_DEV)
    spread = jnp.repeat(upper_field, 2, axis=0)
    leaf_field = (leaf_far + jnp.einsum('lcm,lkm->lck', spread.astype(jnp.float32), transfer.astype(jnp.float32))).astype(jnp.bfloat16)
    far_part = jnp.einsum('lck,lkp->lcp', leaf_field.astype(jnp.float32), leaf_basis.astype(jnp.float32))

    def near_single(target_points, chosen):
        kernel = matern(target_points.astype(jnp.float32)[None], points[chosen].astype(jnp.float32)).astype(jnp.bfloat16)
        return jnp.einsum('jcs,jts->ct', masked[chosen].astype(jnp.float32), kernel.astype(jnp.float32))
    near_part = blocked(near_single, (points, near_list), 4)
    return jnp.where(point_live[:, None, :], far_part + near_part, 0.0)
```

```python
import math

import jax
import jax.numpy as jnp
from jax import lax
from jax.experimental import pallas as pl
from jax.experimental.pallas import tpu as pltpu
from jax.sharding import PartitionSpec as P

HALO = 4
UNROLL = 16
S_SCALE = math.sqrt(3.0) / 1.5
EXP_SCALE = -S_SCALE / math.log(2.0)
TINY = 1e-12
VMEM = 56 * 1024 * 1024


def norm_rows(coords):
    row = lax.broadcasted_iota(jnp.int32, coords.shape, 0)
    norm = jnp.sum(coords * coords, axis=0, keepdims=True)
    high = norm.astype(jnp.bfloat16).astype(jnp.float32)
    rest = norm - high
    mid = rest.astype(jnp.bfloat16).astype(jnp.float32)
    ones = jnp.where((row >= 4) & (row < 7), 1.0, 0.0)
    return jnp.where(row == 0, high, jnp.where(row == 1, mid, jnp.where(row == 2, rest - mid, ones)))


def source_features(coords):
    return jnp.concatenate([coords, norm_rows(coords)], axis=0)


def target_features(coords):
    return jnp.concatenate([coords * -2.0, pltpu.roll(norm_rows(coords), 4, 0)], axis=0)


def matern(square):
    bounded = jnp.maximum(square, TINY)
    dist = bounded * lax.rsqrt(bounded)
    return ((1.0 + dist * S_SCALE) * jnp.exp2(dist * EXP_SCALE)).astype(jnp.bfloat16)


def prepare(count_ref, point_ref, value_ref, basis_ref, transfer_ref, feat_ref, masked_ref, coef_ref, upper_ref):
    leaves, columns, leaf_size = value_ref.shape
    base = pl.program_id(0) * leaves
    lane = lax.broadcasted_iota(jnp.int32, (columns, leaf_size), 1)
    parent = None
    for u in range(leaves):
        feat_ref[u] = source_features(point_ref[u].astype(jnp.float32)).astype(jnp.bfloat16)
        kept = jnp.where(lane < count_ref[base + u], value_ref[u].astype(jnp.float32), 0.0)
        kept = kept.astype(jnp.bfloat16)
        masked_ref[u] = kept
        coef = lax.dot_general(
            kept, basis_ref[u], (((1,), (1,)), ((), ())), preferred_element_type=jnp.float32
        ).astype(jnp.bfloat16)
        coef_ref[u] = coef
        term = jnp.dot(coef, transfer_ref[u], preferred_element_type=jnp.float32)
        if u % 2 == 0:
            parent = term
        else:
            upper_ref[u // 2] = (parent + term).astype(jnp.bfloat16)


def near_kernel(near, offset, ids_ref, feat_ref, val_ref, _, out_ref, done_ref):
    done_ref[0] = 0
    leaves = out_ref.shape[0]
    pair = math.gcd(leaves, 2)

    def group(g, _):
        for u in range(pair):
            l = g * pair + u
            base = (offset + l) * near
            own = feat_ref[ids_ref[base]].astype(jnp.float32)
            target = jnp.concatenate([own[0:8] * -2.0, pltpu.roll(own[8:16], 4, 0)], axis=0)
            target = target.astype(jnp.bfloat16)
            total = None
            for j in range(near):
                q = ids_ref[base + j]
                square = lax.dot_general(
                    feat_ref[q],
                    target,
                    (((0,), (0,)), ((), ())),
                    preferred_element_type=jnp.float32,
                )
                part = jnp.dot(val_ref[q], matern(square), preferred_element_type=jnp.float32)
                total = part if total is None else total + part
            out_ref[l] = total
        return 0

    lax.fori_loop(0, leaves // pair, group, 0)


def pick_pair(row_ref, half_ref, rows_ref, first, lane):
    rank = rows_ref.shape[2] // 2
    left = rows_ref[row_ref[first]].astype(jnp.float32)
    right = rows_ref[row_ref[first + 1]].astype(jnp.float32)
    left = pltpu.roll(left, half_ref[first] * rank, 1)
    right = pltpu.roll(right, (1 - half_ref[first + 1]) * rank, 1)
    return jnp.where(lane < rank, left, right)


def far_kernel_matrix(far, row_ref, half_ref, target_ref, rows_ref, out_ref):
    lane = lax.broadcasted_iota(jnp.int32, rows_ref.shape[1:], 1)
    unroll = out_ref.shape[0]
    for u in range(unroll):
        base = (pl.program_id(0) * unroll + u) * far
        sources = [
            source_features(pick_pair(row_ref, half_ref, rows_ref, base + f, lane)).astype(jnp.bfloat16)
            for f in range(0, far, 2)
        ]
        target = target_features(target_ref[u].astype(jnp.float32)).T.astype(jnp.bfloat16)
        square = jnp.dot(
            target, jnp.concatenate(sources, axis=1), preferred_element_type=jnp.float32
        )
        out_ref[u] = matern(square)


def far_apply(far, row_ref, half_ref, matrix_ref, rows_ref, out_ref):
    lane = lax.broadcasted_iota(jnp.int32, rows_ref.shape[1:], 1)
    unroll = out_ref.shape[0]
    for u in range(unroll):
        base = (pl.program_id(0) * unroll + u) * far
        coefs = [
            pick_pair(row_ref, half_ref, rows_ref, base + f, lane).astype(jnp.bfloat16)
            for f in range(0, far, 2)
        ]
        out_ref[u] = lax.dot_general(
            jnp.concatenate(coefs, axis=1),
            matrix_ref[u],
            (((1,), (1,)), ((), ())),
            preferred_element_type=jnp.float32,
        )


def paired(bundle):
    half = bundle.shape[0] // 2
    return jnp.concatenate([bundle[:half], bundle[half:]], axis=2)


def body(
    points,
    values,
    counts,
    leaf_basis,
    transfer,
    leaf_skeleton,
    upper_skeleton,
    near_list,
    far_owner,
    far_local,
    upper_owner,
    upper_local,
):
    leaf_dev, _, leaf_size = points.shape
    columns = values.shape[1]
    rank = leaf_basis.shape[1]
    far = far_owner.shape[1]
    near = near_list.shape[1]
    par_dev = leaf_dev // 2
    half = leaf_dev // 2
    upper_half = par_dev // 2
    block = half + upper_half
    count = lax.axis_size("leaf")
    side = lax.axis_index("rhs")
    swap = [(0, 1), (1, 0)]

    smem = pl.BlockSpec(memory_space=pltpu.SMEM)
    vmem = pl.BlockSpec(memory_space=pltpu.VMEM)
    params = pltpu.CompilerParams(vmem_limit_bytes=VMEM)

    group = math.gcd(leaf_dev, UNROLL)
    feats, masked, leaf_coef, upper_coef = pl.pallas_call(
        prepare,
        grid=(leaf_dev // group,),
        in_specs=[
            smem,
            pl.BlockSpec((group, 8, leaf_size), lambda g: (g, 0, 0)),
            pl.BlockSpec((group, columns, leaf_size), lambda g: (g, 0, 0)),
            pl.BlockSpec((group, rank, leaf_size), lambda g: (g, 0, 0)),
            pl.BlockSpec((group, rank, rank), lambda g: (g, 0, 0)),
        ],
        out_specs=[
            pl.BlockSpec((group, 16, leaf_size), lambda g: (g, 0, 0)),
            pl.BlockSpec((group, columns, leaf_size), lambda g: (g, 0, 0)),
            pl.BlockSpec((group, columns, rank), lambda g: (g, 0, 0)),
            pl.BlockSpec((group // 2, columns, rank), lambda g: (g, 0, 0)),
        ],
        out_shape=[
            jax.ShapeDtypeStruct((leaf_dev, 16, leaf_size), jnp.bfloat16),
            jax.ShapeDtypeStruct((leaf_dev, columns, leaf_size), jnp.bfloat16),
            jax.ShapeDtypeStruct((leaf_dev, columns, rank), jnp.bfloat16),
            jax.ShapeDtypeStruct((par_dev, columns, rank), jnp.bfloat16),
        ],
        compiler_params=params,
        name="prepare",
    )(counts, points, values, leaf_basis, transfer)

    skeletons = jnp.concatenate([paired(leaf_skeleton), paired(upper_skeleton)], axis=0)
    piece = block // 2
    packed = jnp.concatenate(
        [
            paired(leaf_coef),
            paired(upper_coef),
            lax.dynamic_slice_in_dim(skeletons, side * piece, piece),
        ],
        axis=0,
    )[None]
    me = lax.axis_index("leaf")

    def across(cells, bits):
        return lax.ppermute(cells, "leaf", [(i, i ^ bits) for i in range(count)])

    def shifted(cells, step, other):
        pairs = [
            ((i * 2 + s), (i + step) * 2 + (s ^ other))
            for i in range(count)
            for s in range(2)
            if 0 <= i + step < count
        ]
        return lax.ppermute(cells, ("leaf", "rhs"), pairs)

    tail, head = slice(leaf_dev - HALO, leaf_dev), slice(0, HALO)
    before = shifted(jnp.concatenate([feats[tail], masked[tail]], axis=1), 1, 0)
    after = shifted(jnp.concatenate([feats[head], masked[head]], axis=1), -1, 0)
    partner = jnp.concatenate(
        [shifted(masked[tail], 1, 1), lax.ppermute(masked, "rhs", swap), shifted(masked[head], -1, 1)],
        axis=0,
    )
    feats = jnp.concatenate([before[:, :16], feats, after[:, :16]], axis=0)
    own_vals = jnp.concatenate([before[:, 16:], masked, after[:, 16:]], axis=0)
    vals = jnp.concatenate([own_vals, partner], axis=1)

    first_leaf = me * leaf_dev - HALO
    start = side * half
    near_ids = (lax.dynamic_slice_in_dim(near_list, start, half) - first_leaf).reshape(-1)

    def after_piece(done, cells):
        return jnp.where(done[0] == 0, cells, jnp.zeros_like(cells))

    def near_piece(offset, leaves, follows):
        work = leaves * near * leaf_size * leaf_size
        return pl.pallas_call(
            lambda *refs: near_kernel(near, offset, *refs),
            out_shape=[
                jax.ShapeDtypeStruct((leaves, 2 * columns, leaf_size), jnp.float32),
                jax.ShapeDtypeStruct((1,), jnp.int32),
            ],
            in_specs=[smem, vmem, vmem, pl.BlockSpec(memory_space=pl.ANY)],
            out_specs=[vmem, smem],
            compiler_params=params,
            cost_estimate=pl.CostEstimate(
                flops=work * 64, bytes_accessed=1 << 22, transcendentals=work * 2
            ),
            name="near_field",
        )(near_ids, feats, vals, follows)

    cuts = [0, half // 4, half * 5 // 8, half * 7 // 8, half]
    sizes = [cuts[i + 1] - cuts[i] for i in range(4)]
    if count == 16:
        apart = [across(packed, bits) for bits in (4, 8, 12)]
        near0, done = near_piece(cuts[0], sizes[0], packed)
        column = after_piece(done, jnp.concatenate([packed] + apart, axis=0))
        along_x, along_y = across(column, 1), across(column, 2)
        near1, done = near_piece(cuts[1], sizes[1], column)
        from_x, from_y = after_piece(done, along_x[:2]), after_piece(done, along_y[2:])
        diagonal = [across(from_x, 2), across(from_y, 1)]
        near2, done = near_piece(cuts[2], sizes[2], from_y)
        everything = jnp.concatenate([column, along_x, along_y] + diagonal, axis=0)

        def position(owner):
            apart_bits = owner ^ me
            return (apart_bits & 3) * 4 + (apart_bits >> 2)

    else:
        near0, near1, near2 = [near_piece(cuts[i], sizes[i], packed)[0] for i in range(3)]
        done = jnp.zeros((1,), jnp.int32)
        everything = lax.all_gather(packed, "leaf", axis=0, tiled=True)

        def position(owner):
            return owner
    coefs = everything[:, :block].reshape(count * block, columns, 2 * rank)
    half_skel = after_piece(done, everything[:, block:]).reshape(count * piece, 8, 2 * rank)
    skeletons = jnp.concatenate([half_skel, lax.ppermute(half_skel, "rhs", swap)], axis=0)
    near3, _ = near_piece(cuts[3], sizes[3], half_skel)
    near_half = jnp.concatenate([near0, near1, near2, near3], axis=0)
    mine = near_half[:, :columns]
    other = lax.ppermute(near_half[:, columns:], "rhs", swap)
    near_part = jnp.where(
        side == 0,
        jnp.concatenate([mine, other], axis=0),
        jnp.concatenate([other, mine], axis=0),
    )
    live = lax.broadcasted_iota(jnp.int32, (leaf_dev, leaf_size), 1) < counts[:, None]

    targets = jnp.concatenate([leaf_skeleton, upper_skeleton], axis=0)
    row_in_block = jnp.concatenate(
        [far_local % half, half + upper_local % upper_half], axis=0
    ).reshape(-1)
    place = position(jnp.concatenate([far_owner, upper_owner], axis=0).reshape(-1))
    row_ids = place * block + row_in_block
    skel_ids = (
        jnp.where(row_in_block // piece == side, 0, count * piece)
        + place * piece
        + row_in_block % piece
    )
    half_ids = jnp.concatenate([far_local // half, upper_local // upper_half], axis=0).reshape(-1)
    clusters = leaf_dev + par_dev
    unroll = math.gcd(clusters, UNROLL)
    pairs_far = clusters * far * rank * rank
    matrix_spec = pl.BlockSpec((unroll, rank, far * rank), lambda g: (g, 0, 0))
    matrix = pl.pallas_call(
        lambda *refs: far_kernel_matrix(far, *refs),
        grid=(clusters // unroll,),
        out_shape=jax.ShapeDtypeStruct((clusters, rank, far * rank), jnp.bfloat16),
        in_specs=[smem, smem, pl.BlockSpec((unroll, 8, rank), lambda g: (g, 0, 0)), vmem],
        out_specs=matrix_spec,
        compiler_params=params,
        cost_estimate=pl.CostEstimate(
            flops=pairs_far * 64, bytes_accessed=1 << 24, transcendentals=pairs_far * 2
        ),
        name="far_matrices",
    )(skel_ids, half_ids, targets, skeletons)
    field = pl.pallas_call(
        lambda *refs: far_apply(far, *refs),
        grid=(clusters // unroll,),
        out_shape=jax.ShapeDtypeStruct((clusters, columns, rank), jnp.float32),
        in_specs=[smem, smem, matrix_spec, vmem],
        out_specs=pl.BlockSpec((unroll, columns, rank), lambda g: (g, 0, 0)),
        compiler_params=params,
        cost_estimate=pl.CostEstimate(
            flops=pairs_far * 16, bytes_accessed=1 << 24, transcendentals=0
        ),
        name="far_apply",
    )(row_ids, half_ids, matrix, coefs)

    spread = jnp.repeat(field[leaf_dev:].astype(jnp.bfloat16), 2, axis=0)
    leaf_field = (
        field[:leaf_dev]
        + jnp.einsum("lcm,lkm->lck", spread, transfer, preferred_element_type=jnp.float32)
    ).astype(jnp.bfloat16)
    far_part = jnp.einsum(
        "lck,lkp->lcp", leaf_field, leaf_basis, preferred_element_type=jnp.float32
    )
    return jnp.where(live[:, None, :], far_part + near_part, 0.0)


def solution(mesh):
    return jax.shard_map(
        body,
        mesh=mesh,
        in_specs=(
            P("leaf", None, None),
            P("leaf", "rhs", None),
            P("leaf"),
            P("leaf", None, None),
            P("leaf", None, None),
            P("leaf", None, None),
            P("leaf", None, None),
            P("leaf", None),
            P("leaf", None),
            P("leaf", None),
            P("leaf", None),
            P("leaf", None),
        ),
        out_specs=P("leaf", "rhs", None),
        check_vma=False,
    )
```

```python
import math

import jax
import jax.numpy as jnp
from jax import lax
from jax.experimental import pallas as pl
from jax.experimental.pallas import tpu as pltpu
from jax.sharding import PartitionSpec as P

HALO = 4
UNROLL = 16
S_SCALE = math.sqrt(3.0) / 1.5
EXP_SCALE = -S_SCALE / math.log(2.0)
TINY = 1e-12
VMEM = 56 * 1024 * 1024


def norm_rows(coords):
    row = lax.broadcasted_iota(jnp.int32, coords.shape, 0)
    norm = jnp.sum(coords * coords, axis=0, keepdims=True)
    high = norm.astype(jnp.bfloat16).astype(jnp.float32)
    rest = norm - high
    mid = rest.astype(jnp.bfloat16).astype(jnp.float32)
    ones = jnp.where((row >= 4) & (row < 7), 1.0, 0.0)
    return jnp.where(row == 0, high, jnp.where(row == 1, mid, jnp.where(row == 2, rest - mid, ones)))


def source_features(coords):
    return jnp.concatenate([coords, norm_rows(coords)], axis=0)


def target_features(coords):
    return jnp.concatenate([coords * -2.0, pltpu.roll(norm_rows(coords), 4, 0)], axis=0)


def matern(square):
    bounded = jnp.maximum(square, TINY)
    dist = bounded * lax.rsqrt(bounded)
    return ((1.0 + dist * S_SCALE) * jnp.exp2(dist * EXP_SCALE)).astype(jnp.bfloat16)


def prepare(count_ref, point_ref, value_ref, feat_ref, masked_ref):
    leaves, columns, leaf_size = value_ref.shape
    base = pl.program_id(0) * leaves
    lane = lax.broadcasted_iota(jnp.int32, (columns, leaf_size), 1)
    for u in range(leaves):
        feat_ref[u] = source_features(point_ref[u].astype(jnp.float32)).astype(jnp.bfloat16)
        kept = jnp.where(lane < count_ref[base + u], value_ref[u].astype(jnp.float32), 0.0)
        masked_ref[u] = kept.astype(jnp.bfloat16)


def near_kernel(near, offset, ids_ref, feat_ref, val_ref, _, out_ref, done_ref):
    done_ref[0] = 0
    leaves = out_ref.shape[0]
    pair = math.gcd(leaves, 2)

    def group(g, _):
        for u in range(pair):
            l = g * pair + u
            base = offset + l
            own = feat_ref[ids_ref[base, 0]].astype(jnp.float32)
            target = jnp.concatenate([own[0:8] * -2.0, pltpu.roll(own[8:16], 4, 0)], axis=0)
            target = target.astype(jnp.bfloat16)
            total = None
            for j in range(near):
                q = ids_ref[base, j]
                square = lax.dot_general(
                    feat_ref[q],
                    target,
                    (((0,), (0,)), ((), ())),
                    preferred_element_type=jnp.float32,
                )
                part = jnp.dot(val_ref[q], matern(square), preferred_element_type=jnp.float32)
                total = part if total is None else total + part
            out_ref[l] = total
        return 0

    lax.fori_loop(0, leaves // pair, group, 0)


def side_by_side(left, left_half, right, right_half, lane):
    rank = left.shape[1] // 2
    left = pltpu.roll(left.astype(jnp.float32), left_half * rank, 1)
    right = pltpu.roll(right.astype(jnp.float32), (1 - right_half) * rank, 1)
    return jnp.where(lane < rank, left, right)


def far_kernel_matrix(far, id_ref, target_ref, own_ref, other_ref, out_ref):
    lane = lax.broadcasted_iota(jnp.int32, own_ref.shape[1:], 1)

    def load(at):
        word = id_ref[at]
        own = own_ref[word >> 16]
        other = other_ref[(word >> 2) & 0x3FFF]
        return jnp.where((word & 2) == 2, own, other), word & 1

    def pair(t, f):
        return side_by_side(*load((t, f)), *load((t, f + 1)), lane)

    unroll = out_ref.shape[0]
    for u in range(unroll):
        base = pl.program_id(0) * unroll + u
        sources = [
            source_features(pair(base, f)).astype(jnp.bfloat16)
            for f in range(0, far, 2)
        ]
        target = target_features(target_ref[u].astype(jnp.float32)).T.astype(jnp.bfloat16)
        square = jnp.dot(
            target, jnp.concatenate(sources, axis=1), preferred_element_type=jnp.float32
        )
        out_ref[u] = matern(square)


def far_apply(far, id_ref, matrix_ref, rows_ref, out_ref):
    lane = lax.broadcasted_iota(jnp.int32, rows_ref.shape[1:], 1)

    def load(at):
        return rows_ref[id_ref[at] >> 1], id_ref[at] & 1

    unroll = out_ref.shape[0]
    for u in range(unroll):
        base = pl.program_id(0) * unroll + u
        coefs = [
            side_by_side(*load((base, f)), *load((base, f + 1)), lane).astype(jnp.bfloat16)
            for f in range(0, far, 2)
        ]
        out_ref[u] = lax.dot_general(
            jnp.concatenate(coefs, axis=1),
            matrix_ref[u],
            (((1,), (1,)), ((), ())),
            preferred_element_type=jnp.float32,
        )


def paired(bundle):
    half = bundle.shape[0] // 2
    return jnp.concatenate([bundle[:half], bundle[half:]], axis=2)


def body(
    points,
    values,
    counts,
    leaf_basis,
    transfer,
    leaf_skeleton,
    upper_skeleton,
    near_list,
    far_owner,
    far_local,
    upper_owner,
    upper_local,
):
    leaf_dev, _, leaf_size = points.shape
    columns = values.shape[1]
    rank = leaf_basis.shape[1]
    far = far_owner.shape[1]
    near = near_list.shape[1]
    par_dev = leaf_dev // 2
    half = leaf_dev // 2
    upper_half = par_dev // 2
    block = half + upper_half
    count = lax.axis_size("leaf")
    side = lax.axis_index("rhs")
    swap = [(0, 1), (1, 0)]

    smem = pl.BlockSpec(memory_space=pltpu.SMEM)
    vmem = pl.BlockSpec(memory_space=pltpu.VMEM)
    params = pltpu.CompilerParams(vmem_limit_bytes=VMEM)

    group = math.gcd(leaf_dev, 2 * UNROLL)
    feats, masked = pl.pallas_call(
        prepare,
        grid=(leaf_dev // group,),
        in_specs=[
            smem,
            pl.BlockSpec((group, 8, leaf_size), lambda g: (g, 0, 0)),
            pl.BlockSpec((group, columns, leaf_size), lambda g: (g, 0, 0)),
        ],
        out_specs=[
            pl.BlockSpec((group, 16, leaf_size), lambda g: (g, 0, 0)),
            pl.BlockSpec((group, columns, leaf_size), lambda g: (g, 0, 0)),
        ],
        out_shape=[
            jax.ShapeDtypeStruct((leaf_dev, 16, leaf_size), jnp.bfloat16),
            jax.ShapeDtypeStruct((leaf_dev, columns, leaf_size), jnp.bfloat16),
        ],
        compiler_params=params,
        name="prepare",
    )(counts, points, values)
    leaf_coef = jnp.einsum(
        "lcp,lkp->lck", masked, leaf_basis, preferred_element_type=jnp.float32
    ).astype(jnp.bfloat16)
    upper_coef = jnp.einsum(
        "pjck,pjkm->pcm",
        leaf_coef.reshape(par_dev, 2, columns, rank),
        transfer.reshape(par_dev, 2, rank, rank),
        preferred_element_type=jnp.float32,
    ).astype(jnp.bfloat16)

    skeletons = jnp.concatenate([paired(leaf_skeleton), paired(upper_skeleton)], axis=0)
    piece = block // 2
    packed = jnp.concatenate(
        [
            paired(leaf_coef),
            paired(upper_coef),
            lax.dynamic_slice_in_dim(skeletons, side * piece, piece),
        ],
        axis=0,
    )[None]
    me = lax.axis_index("leaf")

    def across(cells, bits):
        return lax.ppermute(cells, "leaf", [(i, i ^ bits) for i in range(count)])

    def shifted(cells, step, other):
        pairs = [
            ((i * 2 + s), (i + step) * 2 + (s ^ other))
            for i in range(count)
            for s in range(2)
            if 0 <= i + step < count
        ]
        return lax.ppermute(cells, ("leaf", "rhs"), pairs)

    tail, head = slice(leaf_dev - HALO, leaf_dev), slice(0, HALO)
    before = shifted(jnp.concatenate([feats[tail], masked[tail]], axis=1), 1, 0)
    after = shifted(jnp.concatenate([feats[head], masked[head]], axis=1), -1, 0)
    partner = jnp.concatenate(
        [shifted(masked[tail], 1, 1), lax.ppermute(masked, "rhs", swap), shifted(masked[head], -1, 1)],
        axis=0,
    )
    feats = jnp.concatenate([before[:, :16], feats, after[:, :16]], axis=0)
    own_vals = jnp.concatenate([before[:, 16:], masked, after[:, 16:]], axis=0)
    vals = jnp.concatenate([own_vals, partner], axis=1)

    first_leaf = me * leaf_dev - HALO
    start = side * half
    near_ids = lax.dynamic_slice_in_dim(near_list, start, half) - first_leaf

    def after_piece(done, cells):
        return jnp.where(done[0] == 0, cells, jnp.zeros_like(cells))

    def near_piece(offset, leaves, follows):
        work = leaves * near * leaf_size * leaf_size
        return pl.pallas_call(
            lambda *refs: near_kernel(near, offset, *refs),
            out_shape=[
                jax.ShapeDtypeStruct((leaves, 2 * columns, leaf_size), jnp.float32),
                jax.ShapeDtypeStruct((1,), jnp.int32),
            ],
            in_specs=[smem, vmem, vmem, pl.BlockSpec(memory_space=pl.ANY)],
            out_specs=[vmem, smem],
            compiler_params=params,
            cost_estimate=pl.CostEstimate(
                flops=work * 64, bytes_accessed=1 << 22, transcendentals=work * 2
            ),
            name="near_field",
        )(near_ids, feats, vals, follows)

    cuts = [0, half // 4, half * 5 // 8, half * 7 // 8, half]
    sizes = [cuts[i + 1] - cuts[i] for i in range(4)]
    if count == 16:
        apart = [across(packed, bits) for bits in (4, 8, 12)]
        near0, done = near_piece(cuts[0], sizes[0], packed)
        column = after_piece(done, jnp.concatenate([packed] + apart, axis=0))
        along_x, along_y = across(column, 1), across(column, 2)
        near1, done = near_piece(cuts[1], sizes[1], column)
        from_x, from_y = after_piece(done, along_x[:2]), after_piece(done, along_y[2:])
        diagonal = [across(from_x, 2), across(from_y, 1)]
        near2, done = near_piece(cuts[2], sizes[2], from_y)
        everything = jnp.concatenate([column, along_x, along_y] + diagonal, axis=0)

        def position(owner):
            apart_bits = owner ^ me
            return (apart_bits & 3) * 4 + (apart_bits >> 2)

    else:
        near0, near1, near2 = [near_piece(cuts[i], sizes[i], packed)[0] for i in range(3)]
        done = jnp.zeros((1,), jnp.int32)
        everything = lax.all_gather(packed, "leaf", axis=0, tiled=True)

        def position(owner):
            return owner
    half_skel = after_piece(done, everything[:, block:]).reshape(count * piece, 8, 2 * rank)
    other_skel = lax.ppermute(half_skel, "rhs", swap)
    everything = everything.reshape(count * (block + piece), 8, 2 * rank)
    near3, _ = near_piece(cuts[3], sizes[3], half_skel)
    near_half = jnp.concatenate([near0, near1, near2, near3], axis=0)
    mine = near_half[:, :columns]
    other = lax.ppermute(near_half[:, columns:], "rhs", swap)
    near_part = jnp.where(
        side == 0,
        jnp.concatenate([mine, other], axis=0),
        jnp.concatenate([other, mine], axis=0),
    )
    live = lax.broadcasted_iota(jnp.int32, (leaf_dev, leaf_size), 1) < counts[:, None]

    targets = jnp.concatenate([leaf_skeleton, upper_skeleton], axis=0)
    row_in_block = jnp.concatenate([far_local % half, half + upper_local % upper_half], axis=0)
    place = position(jnp.concatenate([far_owner, upper_owner], axis=0))
    row_ids = place * (block + piece) + row_in_block
    own_ids = place * (block + piece) + block + row_in_block % piece
    other_ids = place * piece + row_in_block % piece
    own_flags = jnp.where(row_in_block // piece == side, 1, 0)
    half_ids = jnp.concatenate([far_local // half, upper_local // upper_half], axis=0)
    skel_ids = (own_ids << 16) + (other_ids << 2) + (own_flags << 1) + half_ids
    coef_ids = row_ids * 2 + half_ids
    clusters = leaf_dev + par_dev
    unroll = math.gcd(clusters, UNROLL)
    pairs_far = clusters * far * rank * rank
    matrix_spec = pl.BlockSpec((unroll, rank, far * rank), lambda g: (g, 0, 0))
    matrix = pl.pallas_call(
        lambda *refs: far_kernel_matrix(far, *refs),
        grid=(clusters // unroll,),
        out_shape=jax.ShapeDtypeStruct((clusters, rank, far * rank), jnp.bfloat16),
        in_specs=[smem, pl.BlockSpec((unroll, 8, rank), lambda g: (g, 0, 0)), vmem, vmem],
        out_specs=matrix_spec,
        compiler_params=params,
        cost_estimate=pl.CostEstimate(
            flops=pairs_far * 64, bytes_accessed=1 << 24, transcendentals=pairs_far * 2
        ),
        name="far_matrices",
    )(skel_ids, targets, everything, other_skel)
    field = pl.pallas_call(
        lambda *refs: far_apply(far, *refs),
        grid=(clusters // unroll,),
        out_shape=jax.ShapeDtypeStruct((clusters, columns, rank), jnp.float32),
        in_specs=[smem, matrix_spec, vmem],
        out_specs=pl.BlockSpec((unroll, columns, rank), lambda g: (g, 0, 0)),
        compiler_params=params,
        cost_estimate=pl.CostEstimate(
            flops=pairs_far * 16, bytes_accessed=1 << 24, transcendentals=0
        ),
        name="far_apply",
    )(coef_ids, matrix, everything)

    spread = jnp.repeat(field[leaf_dev:].astype(jnp.bfloat16), 2, axis=0)
    leaf_field = (
        field[:leaf_dev]
        + jnp.einsum("lcm,lkm->lck", spread, transfer, preferred_element_type=jnp.float32)
    ).astype(jnp.bfloat16)
    far_part = jnp.einsum(
        "lck,lkp->lcp", leaf_field, leaf_basis, preferred_element_type=jnp.float32
    )
    return jnp.where(live[:, None, :], far_part + near_part, 0.0)


def solution(mesh):
    return jax.shard_map(
        body,
        mesh=mesh,
        in_specs=(
            P("leaf", None, None),
            P("leaf", "rhs", None),
            P("leaf"),
            P("leaf", None, None),
            P("leaf", None, None),
            P("leaf", None, None),
            P("leaf", None, None),
            P("leaf", None),
            P("leaf", None),
            P("leaf", None),
            P("leaf", None),
            P("leaf", None),
        ),
        out_specs=P("leaf", "rhs", None),
        check_vma=False,
    )
```

```python
import math

import jax
import jax.numpy as jnp
from jax import lax
from jax.experimental import pallas as pl
from jax.experimental.pallas import tpu as pltpu
from jax.sharding import PartitionSpec as P

HALO = 4
ROWS = 64
UNROLL = 16
S_SCALE = math.sqrt(3.0) / 1.5
EXP_SCALE = -S_SCALE / math.log(2.0)
TINY = 1e-12
VMEM = 56 * 1024 * 1024


def norm_rows(coords):
    row = lax.broadcasted_iota(jnp.int32, coords.shape, 0)
    norm = jnp.sum(coords * coords, axis=0, keepdims=True)
    high = norm.astype(jnp.bfloat16).astype(jnp.float32)
    rest = norm - high
    mid = rest.astype(jnp.bfloat16).astype(jnp.float32)
    ones = jnp.where((row >= 4) & (row < 7), 1.0, 0.0)
    return jnp.where(row == 0, high, jnp.where(row == 1, mid, jnp.where(row == 2, rest - mid, ones)))


def source_features(coords):
    return jnp.concatenate([coords, norm_rows(coords)], axis=0)


def target_features(coords):
    return jnp.concatenate([coords * -2.0, pltpu.roll(norm_rows(coords), 4, 0)], axis=0)


def matern(square):
    bounded = jnp.maximum(square, TINY)
    dist = bounded * lax.rsqrt(bounded)
    return ((1.0 + dist * S_SCALE) * jnp.exp2(dist * EXP_SCALE)).astype(jnp.bfloat16)


def near_kernel(near, ids_ref, point_ref, val_ref, out_ref, done_ref, source_ref):
    done_ref[0] = 0
    sources = point_ref.shape[0]
    leaves = out_ref.shape[0]
    wide = math.gcd(sources, 8)
    pair = math.gcd(leaves, 2)

    def turn(g, _):
        for u in range(wide):
            q = g * wide + u
            rows = source_features(point_ref[q].astype(jnp.float32))
            source_ref[q] = rows.T.astype(jnp.bfloat16)
        return 0

    lax.fori_loop(0, sources // wide, turn, 0)

    def group(g, _):
        for u in range(pair):
            l = g * pair + u
            own = point_ref[ids_ref[l, 0]].astype(jnp.float32)
            target = target_features(own).astype(jnp.bfloat16)
            total = None
            for j in range(near):
                q = ids_ref[l, j]
                blocks = [
                    matern(
                        jnp.dot(
                            source_ref[q, r : r + ROWS], target, preferred_element_type=jnp.float32
                        )
                    )
                    for r in range(0, source_ref.shape[1], ROWS)
                ]
                part = jnp.dot(
                    val_ref[q], jnp.concatenate(blocks, axis=0), preferred_element_type=jnp.float32
                )
                total = part if total is None else total + part
            out_ref[l] = total
        return 0

    lax.fori_loop(0, leaves // pair, group, 0)


def side_by_side(left, left_half, right, right_half, lane):
    rank = left.shape[1] // 2
    left = pltpu.roll(left.astype(jnp.float32), left_half * rank, 1)
    right = pltpu.roll(right.astype(jnp.float32), (1 - right_half) * rank, 1)
    return jnp.where(lane < rank, left, right)


def far_kernel_matrix(far, id_ref, target_ref, own_ref, other_ref, out_ref):
    lane = lax.broadcasted_iota(jnp.int32, own_ref.shape[1:], 1)

    def load(at):
        word = id_ref[at]
        own = own_ref[word >> 16]
        other = other_ref[(word >> 2) & 0x3FFF]
        return jnp.where((word & 2) == 2, own, other), word & 1

    def pair(t, f):
        return side_by_side(*load((t, f)), *load((t, f + 1)), lane)

    unroll = out_ref.shape[0]
    for u in range(unroll):
        base = pl.program_id(0) * unroll + u
        sources = [
            source_features(pair(base, f)).astype(jnp.bfloat16)
            for f in range(0, far, 2)
        ]
        target = target_features(target_ref[u].astype(jnp.float32)).T.astype(jnp.bfloat16)
        square = jnp.dot(
            target, jnp.concatenate(sources, axis=1), preferred_element_type=jnp.float32
        )
        out_ref[u] = matern(square)


def far_apply(far, id_ref, matrix_ref, rows_ref, out_ref):
    lane = lax.broadcasted_iota(jnp.int32, rows_ref.shape[1:], 1)

    def load(at):
        return rows_ref[id_ref[at] >> 1], id_ref[at] & 1

    unroll = out_ref.shape[0]
    for u in range(unroll):
        base = pl.program_id(0) * unroll + u
        coefs = [
            side_by_side(*load((base, f)), *load((base, f + 1)), lane).astype(jnp.bfloat16)
            for f in range(0, far, 2)
        ]
        out_ref[u] = lax.dot_general(
            jnp.concatenate(coefs, axis=1),
            matrix_ref[u],
            (((1,), (1,)), ((), ())),
            preferred_element_type=jnp.float32,
        )


def paired(bundle):
    half = bundle.shape[0] // 2
    return jnp.concatenate([bundle[:half], bundle[half:]], axis=2)


def body(
    points,
    values,
    counts,
    leaf_basis,
    transfer,
    leaf_skeleton,
    upper_skeleton,
    near_list,
    far_owner,
    far_local,
    upper_owner,
    upper_local,
):
    leaf_dev, _, leaf_size = points.shape
    columns = values.shape[1]
    rank = leaf_basis.shape[1]
    far = far_owner.shape[1]
    near = near_list.shape[1]
    par_dev = leaf_dev // 2
    half = leaf_dev // 2
    upper_half = par_dev // 2
    block = half + upper_half
    count = lax.axis_size("leaf")
    side = lax.axis_index("rhs")
    swap = [(0, 1), (1, 0)]

    live = lax.broadcasted_iota(jnp.int32, (leaf_dev, leaf_size), 1) < counts[:, None]
    masked = jnp.where(live[:, None, :], values, jnp.zeros_like(values))

    def shifted(cells, step):
        if step > 0:
            pairs = [(i, i + 1) for i in range(count - 1)]
            return lax.ppermute(cells[leaf_dev - HALO :], "leaf", pairs)
        pairs = [(i + 1, i) for i in range(count - 1)]
        return lax.ppermute(cells[:HALO], "leaf", pairs)

    bundle = jnp.concatenate([points, masked], axis=1)
    extended = jnp.concatenate([shifted(bundle, 1), bundle, shifted(bundle, -1)], axis=0)
    own_vals = extended[:, 8:]
    vals = jnp.concatenate([own_vals, lax.ppermute(own_vals, "rhs", swap)], axis=1)

    leaf_coef = jnp.einsum(
        "lcp,lkp->lck", masked, leaf_basis, preferred_element_type=jnp.float32
    ).astype(jnp.bfloat16)
    upper_coef = jnp.einsum(
        "pjck,pjkm->pcm",
        leaf_coef.reshape(par_dev, 2, columns, rank),
        transfer.reshape(par_dev, 2, rank, rank),
        preferred_element_type=jnp.float32,
    ).astype(jnp.bfloat16)
    skeletons = jnp.concatenate([paired(leaf_skeleton), paired(upper_skeleton)], axis=0)
    piece = block // 2
    packed = jnp.concatenate(
        [
            paired(leaf_coef),
            paired(upper_coef),
            lax.dynamic_slice_in_dim(skeletons, side * piece, piece),
        ],
        axis=0,
    )
    everything = lax.all_gather(packed, "leaf", axis=0, tiled=True)
    first_leaf = lax.axis_index("leaf") * leaf_dev - HALO
    start = side * half
    near_ids = (lax.dynamic_slice_in_dim(near_list, start, half) - first_leaf)
    smem = pl.BlockSpec(memory_space=pltpu.SMEM)
    vmem = pl.BlockSpec(memory_space=pltpu.VMEM)
    pairs_near = half * near * leaf_size * leaf_size
    near_half, done = pl.pallas_call(
        lambda *refs: near_kernel(near, *refs),
        out_shape=[
            jax.ShapeDtypeStruct((half, 2 * columns, leaf_size), jnp.float32),
            jax.ShapeDtypeStruct((1,), jnp.int32),
        ],
        in_specs=[smem, vmem, vmem],
        out_specs=[vmem, smem],
        scratch_shapes=[pltpu.VMEM((leaf_dev + 2 * HALO, leaf_size, 16), jnp.bfloat16)],
        compiler_params=pltpu.CompilerParams(vmem_limit_bytes=VMEM),
        cost_estimate=pl.CostEstimate(
            flops=pairs_near * 64, bytes_accessed=1 << 22, transcendentals=pairs_near * 2
        ),
        name="near_field",
    )(near_ids, extended[:, :8], vals)
    own_skel = everything.reshape(count, block + piece, 8, 2 * rank)[:, block:]
    own_skel = jnp.where(done[0] == 0, own_skel, jnp.zeros_like(own_skel))
    other_skel = lax.ppermute(own_skel, "rhs", swap).reshape(count * piece, 8, 2 * rank)
    mine = near_half[:, :columns]
    other = lax.ppermute(near_half[:, columns:], "rhs", swap)
    near_part = jnp.where(
        side == 0,
        jnp.concatenate([mine, other], axis=0),
        jnp.concatenate([other, mine], axis=0),
    )

    targets = jnp.concatenate([leaf_skeleton, upper_skeleton], axis=0)
    row_in_block = jnp.concatenate([far_local % half, half + upper_local % upper_half], axis=0)
    place = jnp.concatenate([far_owner, upper_owner], axis=0)
    row_ids = place * (block + piece) + row_in_block
    own_ids = place * (block + piece) + block + row_in_block % piece
    other_ids = place * piece + row_in_block % piece
    own_flags = jnp.where(row_in_block // piece == side, 1, 0)
    half_ids = jnp.concatenate([far_local // half, upper_local // upper_half], axis=0)
    skel_ids = (own_ids << 16) + (other_ids << 2) + (own_flags << 1) + half_ids
    coef_ids = row_ids * 2 + half_ids
    clusters = leaf_dev + par_dev
    unroll = math.gcd(clusters, UNROLL)
    pairs_far = clusters * far * rank * rank
    params = pltpu.CompilerParams(vmem_limit_bytes=VMEM)
    matrix_spec = pl.BlockSpec((unroll, rank, far * rank), lambda g: (g, 0, 0))
    matrix = pl.pallas_call(
        lambda *refs: far_kernel_matrix(far, *refs),
        grid=(clusters // unroll,),
        out_shape=jax.ShapeDtypeStruct((clusters, rank, far * rank), jnp.bfloat16),
        in_specs=[smem, pl.BlockSpec((unroll, 8, rank), lambda g: (g, 0, 0)), vmem, vmem],
        out_specs=matrix_spec,
        compiler_params=params,
        cost_estimate=pl.CostEstimate(
            flops=pairs_far * 64, bytes_accessed=1 << 24, transcendentals=pairs_far * 2
        ),
        name="far_matrices",
    )(skel_ids, targets, everything, other_skel)
    field = pl.pallas_call(
        lambda *refs: far_apply(far, *refs),
        grid=(clusters // unroll,),
        out_shape=jax.ShapeDtypeStruct((clusters, columns, rank), jnp.float32),
        in_specs=[smem, matrix_spec, vmem],
        out_specs=pl.BlockSpec((unroll, columns, rank), lambda g: (g, 0, 0)),
        compiler_params=params,
        cost_estimate=pl.CostEstimate(
            flops=pairs_far * 16, bytes_accessed=1 << 24, transcendentals=0
        ),
        name="far_apply",
    )(coef_ids, matrix, everything)

    spread = jnp.repeat(field[leaf_dev:].astype(jnp.bfloat16), 2, axis=0)
    leaf_field = (
        field[:leaf_dev]
        + jnp.einsum("lcm,lkm->lck", spread, transfer, preferred_element_type=jnp.float32)
    ).astype(jnp.bfloat16)
    far_part = jnp.einsum(
        "lck,lkp->lcp", leaf_field, leaf_basis, preferred_element_type=jnp.float32
    )
    return jnp.where(live[:, None, :], far_part + near_part, 0.0)


def solution(mesh):
    return jax.shard_map(
        body,
        mesh=mesh,
        in_specs=(
            P("leaf", None, None),
            P("leaf", "rhs", None),
            P("leaf"),
            P("leaf", None, None),
            P("leaf", None, None),
            P("leaf", None, None),
            P("leaf", None, None),
            P("leaf", None),
            P("leaf", None),
            P("leaf", None),
            P("leaf", None),
            P("leaf", None),
        ),
        out_specs=P("leaf", "rhs", None),
        check_vma=False,
    )
```
